512 devices in a mesh: ctx: 64 (over y, z), uly: 8 (over x, core).
Axes of the slice: x: 4, y: 4, z: 16, core: 2. Of those that a mesh axis runs over, the one named last changes fastest.
Arguments:
- lin_query: bfloat16 [32768, 4096], P(('ctx', 'uly')), may hold values from -5 to 5
- lin_key: bfloat16 [32768, 4096], P(('ctx', 'uly')), may hold values from -5 to 5
- lin_value: bfloat16 [32768, 4096], P(('ctx', 'uly')), may hold values from -60 to 60
- log_decay: bfloat16 [32768, 32], P(('ctx', 'uly')), may hold values from 0 to 1
- norm_gain: float32 [4096], P('uly'), may hold values from 0.25 to 1.75
- doc_lengths: int32 [64], replicated, may hold values from 1 to 1024, 32768 in all
- att_query: bfloat16 [32768, 4096], P(('ctx', 'uly')), may hold values from -6 to 6
- att_key: bfloat16 [32768, 1024], P(('ctx', 'uly')), may hold values from -6 to 6
- att_value: bfloat16 [32768, 1024], P(('ctx', 'uly')), may hold values from -5 to 5
Outputs:
- lin_out: bfloat16 [32768, 4096], P('ctx', 'uly')
- att_out: bfloat16 [32768, 4096], P('ctx', 'uly')
The draws below stay inside these ranges and needn't reach their ends.
Inputs may be any that keep to these rules, and one draw needn't show every extreme that they name: `doc_lengths`: documents follow one another from position 0 and fill the sequence; the longest has exactly 1024 positions.
All inputs are finite; a program needn't handle non-finite values.
Results may differ from the reference program's by a relative error of at most 0.008.
Values may be sent and summed in bfloat16 or wider, within the bound.
No kernel may reach another device: no remote copies, remote signals or barrier semaphores. Data moves between devices by JAX's collectives and lax.ppermute only.
A program may use at most 128 MiB of HBM per device.

```python
import math
import jax
import jax.numpy as jnp
import numpy as np
from jax import lax

HEAD = 128
LINEAR_HEADS = 32
HQ = 32
HK = 8
TOK_DEV = 64
BLOCK = 512
SEQUENCE_LENGTH = 32768
MOST = 1024
DOCS = 64


def draw_log_decay(key, part):
    key = jax.random.fold_in(key, 41)
    random_key_parts = jax.random.split(key, 7)
    slow_share = 0.5
    slow_heads = jax.random.uniform(random_key_parts[0], (LINEAR_HEADS,)) < slow_share
    slow_rate = jnp.exp(jax.random.uniform(random_key_parts[1], (LINEAR_HEADS,), minval=math.log(math.log(2.0) / (8.0 * MOST)), maxval=math.log(math.log(2.0) / MOST)))
    quick_decay_value = jnp.exp(jax.random.uniform(random_key_parts[2], (LINEAR_HEADS,), minval=math.log(math.log(10.0) / 50.0), maxval=math.log(math.log(10.0) / 30.0)))
    base_rate = jnp.where(slow_heads, slow_rate, quick_decay_value)
    group_count = SEQUENCE_LENGTH // TOK_DEV
    group_factor = jnp.exp(jax.random.uniform(random_key_parts[3], (group_count, 1, LINEAR_HEADS), minval=math.log(0.5), maxval=math.log(2.0)))
    token_factor = jnp.exp(jax.random.uniform(random_key_parts[4], (group_count, TOK_DEV, LINEAR_HEADS), minval=math.log(0.7), maxval=math.log(1.4)))
    head_decay_values = (base_rate * group_factor * token_factor).reshape(SEQUENCE_LENGTH, LINEAR_HEADS)
    surge_spans = jax.random.uniform(random_key_parts[5], (SEQUENCE_LENGTH, LINEAR_HEADS)) < 16.0 / SEQUENCE_LENGTH
    surge_additional = jax.random.uniform(random_key_parts[6], (SEQUENCE_LENGTH, LINEAR_HEADS), minval=-math.log(0.8), maxval=-math.log(0.5))
    return jnp.where(surge_spans, head_decay_values + surge_additional, head_decay_values).astype(jnp.bfloat16)


def draw_lin_value(key, part):
    key = jax.random.fold_in(key, 53)
    random_key_parts = jax.random.split(key, 3)
    row_width = LINEAR_HEADS * HEAD
    base_draw = jnp.clip(jax.random.normal(random_key_parts[0], (SEQUENCE_LENGTH, row_width)), -4.5, 4.5)
    row_scale = jnp.exp(jax.random.uniform(random_key_parts[1], (SEQUENCE_LENGTH, 1), minval=math.log(0.3), maxval=math.log(3.0)))
    column_scale = jnp.exp(jax.random.uniform(random_key_parts[2], (1, row_width), minval=math.log(0.3), maxval=math.log(3.0)))
    return (base_draw * row_scale * column_scale).astype(jnp.bfloat16)


def draw_att_query(key, part):
    base_draw = jnp.clip(jax.random.normal(jax.random.fold_in(key, 1), (SEQUENCE_LENGTH, HQ * HEAD)), -4.5, 4.5)
    return base_draw.astype(jnp.bfloat16)


def draw_att_key(key, part):
    base_draw = jnp.clip(jax.random.normal(jax.random.fold_in(key, 2), (SEQUENCE_LENGTH, HK * HEAD)), -4.5, 4.5)
    return base_draw.astype(jnp.bfloat16)


def block_levels(rng, dims, shards, low, high):
    gain, own = 1.0, jax.random.fold_in(rng, 6)
    for position, shards_of in shards:
        heights = jnp.exp(jax.random.uniform(jax.random.fold_in(own, position), (shards_of,), jnp.float32, low / len(shards), high / len(shards)))
        gain = gain * jnp.repeat(heights, dims[position] // shards_of).reshape([-1 if axis == position else 1 for axis in range(len(dims))])
    return gain


def length_profile(count, total, reach, skew):
    portions = [(1 << 20) // math.isqrt(grade ** skew) + 1 for grade in range(2, count + 1)]
    surplus, counts = total - reach - (count - 1), [1] * (count - 1)
    while surplus > 0:
        candidates = [i for i in range(count - 1) if counts[i] < reach]
        mass, remaining = sum([portions[i] for i in candidates]), surplus
        for i in candidates:
            addition = min(reach - counts[i], max(1, remaining * portions[i] // mass), surplus)
            counts[i] = counts[i] + addition
            surplus = surplus - addition
    return np.array([reach] + counts)


def uneven_parts(stream_key, number_of, total, reach, skew):
    if number_of == 2:
        one = jax.random.randint(stream_key, (), max(1, total - reach), min(reach, total - 1) + 1)
        return jnp.stack([one, total - one])
    tallies = jnp.asarray(length_profile(number_of, total, reach, skew), jnp.int32)
    couples = (number_of - 1) // 2
    giver, taker = tallies[1:1 + 2 * couples:2], tallies[2:2 + 2 * couples:2]
    slack = jnp.minimum(giver - 1, reach - taker)
    moved = jax.random.randint(jax.random.fold_in(stream_key, 1), (couples,), 0, 1 << 20) % (slack + 1)
    tallies = tallies.at[1:1 + 2 * couples:2].set(giver - moved).at[2:2 + 2 * couples:2].set(taker + moved)
    return tallies[jax.random.permutation(jax.random.fold_in(stream_key, 2), number_of)]


def noise(stream_key, extent, deviation, reach, pieces=(), kind=jnp.bfloat16):
    drawn = deviation * jax.random.normal(stream_key, extent, jnp.float32)
    if pieces:
        drawn = drawn * block_levels(stream_key, extent, pieces, -0.22, 0.18)
    return jnp.clip(drawn, -reach, reach).astype(kind)


def setup_inputs(seed: int = 0) -> dict:
    keys = jax.random.split(jax.random.key(seed), 10)
    lin_query = noise(keys[0], (SEQUENCE_LENGTH, LINEAR_HEADS * HEAD), 1.0, 5.0, ((0, 512),))
    lin_key = noise(keys[1], (SEQUENCE_LENGTH, LINEAR_HEADS * HEAD), 1.0, 5.0, ((0, 512),))
    lin_value = draw_lin_value(jax.random.fold_in(keys[9], 71), 0)
    log_decay = draw_log_decay(jax.random.fold_in(keys[9], 71), 0)
    norm_gain = jnp.clip(1.0 + 0.15 * jax.random.normal(keys[4], (LINEAR_HEADS * HEAD,), jnp.float32), 0.25, 1.75)
    doc_lengths = uneven_parts(keys[5], DOCS, SEQUENCE_LENGTH, MOST, 2).astype(jnp.int32)
    att_query = draw_att_query(jax.random.fold_in(keys[9], 71), 0)
    att_key = draw_att_key(jax.random.fold_in(keys[9], 71), 0)
    att_value = noise(keys[8], (SEQUENCE_LENGTH, HK * HEAD), 1.0, 5.0, ((0, 512),))
    return dict(lin_query=lin_query, lin_key=lin_key, lin_value=lin_value, log_decay=log_decay, norm_gain=norm_gain, doc_lengths=doc_lengths, att_query=att_query, att_key=att_key, att_value=att_value)


def doc_begin(positions, doc_lengths):
    start_pos = (jnp.cumsum(doc_lengths) - doc_lengths).astype(jnp.int32)
    covered = start_pos[None, :] <= positions[:, None]
    return lax.optimization_barrier(jnp.max(jnp.where(covered, start_pos[None, :], 0), axis=1)).astype(jnp.int32)

def rounded(values):
    return lax.optimization_barrier(values.astype(jnp.bfloat16)).astype(jnp.float32)

def lightning_block(query_block, key_block, value_block, decay_block, state, token_begin, block_start, norm_gain):
    offsets = jnp.arange(BLOCK, dtype=jnp.int32)
    decay_sum = jnp.cumsum(decay_block.astype(jnp.float32), axis=0)
    query_map = rounded(jax.nn.silu(query_block.astype(jnp.float32)))
    key_map = rounded(jax.nn.silu(key_block.astype(jnp.float32)))
    values = value_block.astype(jnp.float32)
    scores = jnp.einsum('thd,shd->hts', query_map, key_map)
    allowed = (offsets[None, :] <= offsets[:, None]) & (token_begin[None, :] == token_begin[:, None])
    decay_gap = decay_sum.T[:, :, None] - decay_sum.T[:, None, :]
    weights = jnp.where(allowed[None], jnp.exp(-jnp.where(allowed[None], decay_gap, 0.0)), 0.0)
    inside = jnp.einsum('hts,shd->thd', rounded(weights * scores), values)
    last_begin = token_begin[BLOCK - 1]
    end_weight = jnp.where((token_begin == last_begin)[:, None], jnp.exp(decay_sum - decay_sum[BLOCK - 1][None, :]), 0.0)
    end_state = jnp.einsum('shd,she->hde', rounded(key_map * end_weight[:, :, None]), values)
    block_decay = jnp.where(last_begin < block_start, jnp.exp(-decay_sum[BLOCK - 1]), 0.0)
    entry_decay = jnp.where((token_begin < block_start)[:, None], jnp.exp(-decay_sum), 0.0)
    carried = jnp.einsum('thd,hde->the', query_map, rounded(state)) * entry_decay[:, :, None]
    combined = inside + carried
    normed = combined * lax.rsqrt(lax.optimization_barrier(jnp.mean(combined * combined, axis=-1, keepdims=True)) + 1e-06)
    return (normed * norm_gain.reshape(LINEAR_HEADS, HEAD), end_state, block_decay)

def lightning(lin_query, lin_key, lin_value, log_decay, norm_gain, doc_lengths):
    block_count = SEQUENCE_LENGTH // BLOCK
    offsets = jnp.arange(BLOCK, dtype=jnp.int32)
    queries = lin_query.reshape(block_count, BLOCK, LINEAR_HEADS, HEAD)
    key_rows = lin_key.reshape(block_count, BLOCK, LINEAR_HEADS, HEAD)
    values = lin_value.reshape(block_count, BLOCK, LINEAR_HEADS, HEAD)
    decays = log_decay.reshape(block_count, BLOCK, LINEAR_HEADS)

    def advance(state, inputs):
        query_block, key_block, value_block, decay_block, block_index = inputs
        block_start = (block_index * BLOCK).astype(jnp.int32)
        token_begin = doc_begin(block_start + offsets, doc_lengths)
        normed, end_state, block_decay = lightning_block(query_block, key_block, value_block, decay_block, state, token_begin, block_start, norm_gain)
        return (block_decay[:, None, None] * state + end_state, normed.astype(jnp.bfloat16))
    start_state = jnp.zeros((LINEAR_HEADS, HEAD, HEAD), jnp.float32)
    _, outputs = lax.scan(advance, start_state, (queries, key_rows, values, decays, jnp.arange(block_count, dtype=jnp.int32)))
    return outputs.reshape(SEQUENCE_LENGTH, LINEAR_HEADS * HEAD)

def softmax_layer(att_query, att_key, att_value, doc_lengths):
    block_count = SEQUENCE_LENGTH // BLOCK
    group_size = HQ // HK
    span = MOST + BLOCK
    padded_keys = jnp.concatenate([jnp.zeros((MOST, HK * HEAD), jnp.bfloat16), att_key], axis=0)
    padded_values = jnp.concatenate([jnp.zeros((MOST, HK * HEAD), jnp.bfloat16), att_value], axis=0)
    offsets = jnp.arange(BLOCK, dtype=jnp.int32)
    span_offsets = jnp.arange(span, dtype=jnp.int32)

    def per_block(block_index):
        start = (block_index * BLOCK).astype(jnp.int32)
        queries = lax.dynamic_slice_in_dim(att_query, start, BLOCK, 0).reshape(BLOCK, HK, group_size, HEAD).astype(jnp.float32)
        key_rows = lax.dynamic_slice_in_dim(padded_keys, start, span, 0).reshape(span, HK, HEAD).astype(jnp.float32)
        value_rows = lax.dynamic_slice_in_dim(padded_values, start, span, 0).reshape(span, HK, HEAD).astype(jnp.float32)
        query_position = start + offsets
        key_position = start - MOST + span_offsets
        query_begin = doc_begin(query_position, doc_lengths)
        key_begin = doc_begin(key_position, doc_lengths)
        allowed = (key_position[None, :] <= query_position[:, None]) & (key_position[None, :] >= 0) & (key_begin[None, :] == query_begin[:, None])
        scores = jnp.einsum('tkgd,skd->kgts', queries, key_rows) * HEAD ** (-0.5)
        row_max = lax.optimization_barrier(jnp.max(jnp.where(allowed, scores, -1e+30), axis=-1, keepdims=True))
        weights = jnp.where(allowed, jnp.exp(scores - row_max), 0.0)
        row_total = lax.optimization_barrier(jnp.sum(weights, axis=-1))
        mixed = jnp.einsum('kgts,skd->tkgd', rounded(weights), value_rows)
        return (mixed / jnp.transpose(row_total, (2, 0, 1))[..., None]).reshape(BLOCK, HQ * HEAD).astype(jnp.bfloat16)
    return lax.map(per_block, jnp.arange(block_count, dtype=jnp.int32)).reshape(SEQUENCE_LENGTH, HQ * HEAD)

def reference(lin_query, lin_key, lin_value, log_decay, norm_gain, doc_lengths, att_query, att_key, att_value):
    lin_out = lightning(lin_query, lin_key, lin_value, log_decay, norm_gain, doc_lengths)
    att_out = softmax_layer(att_query, att_key, att_value, doc_lengths)
    return (lin_out, att_out)
```

```python
import functools

import jax
import jax.numpy as jnp
from jax import lax
from jax.experimental import pallas as pl
from jax.experimental.pallas import tpu as pltpu
from jax.sharding import PartitionSpec as P

HEAD = 128
PEERS = 8
TOK = 64
HEADS = 4
BLOCK = PEERS * TOK
REACH = 2 * BLOCK
ROW_TILE = 128
SPAN = REACH + ROW_TILE
DEC_ROW = 10 * TOK
ROWS_A = DEC_ROW + 16
ROWS_B = 12 * TOK
STATE_ROWS = HEADS * HEAD + 16
F32 = jnp.float32
BF16 = jnp.bfloat16
VMEM_LIMIT = 56 * 1024 * 1024


def silu(x):
    return x / (1.0 + jnp.exp(-x))


def call(body, out_shape, scratch=()):
    whole = pl.BlockSpec(memory_space=pltpu.VMEM)
    many = isinstance(out_shape, (tuple, list))
    return pl.pallas_call(
        body,
        out_shape=out_shape,
        out_specs=tuple(whole for _ in out_shape) if many else whole,
        scratch_shapes=list(scratch),
        compiler_params=pltpu.CompilerParams(vmem_limit_bytes=VMEM_LIMIT),
    )


def columns(out, source, first, count):
    for peer in range(PEERS):
        for i in range(count):
            column = (peer * count + i) * HEAD
            out[peer, (first + i) * TOK : (first + i + 1) * TOK, :] = source[:, column : column + HEAD]


def pack_first(k, v, ak, av, decay, out, window):
    columns(out, k, 0, HEADS)
    columns(out, v, 4, HEADS)
    columns(out, ak, 8, 1)
    columns(out, av, 9, 1)
    columns(window, ak, 0, 1)
    columns(window, av, 1, 1)
    turned = jnp.transpose(decay[...].astype(F32))
    turned = jnp.concatenate([turned, jnp.zeros((32, 64), F32)], axis=1)
    for peer in range(PEERS):
        rows = turned[HEADS * peer : HEADS * (peer + 1), :]
        rows = jnp.concatenate([rows, jnp.zeros((12, 128), F32)], axis=0)
        out[peer, DEC_ROW : DEC_ROW + 16, :] = rows.astype(BF16)


def pack_second(q, aq, kv1, kv2, out):
    columns(out, q, 0, HEADS)
    columns(out, aq, 4, HEADS)
    out[:, 8 * TOK : 10 * TOK, :] = kv1[...]
    out[:, 10 * TOK : 12 * TOK, :] = kv2[...]


def begins(lens):
    start = lax.axis_index("ctx") * BLOCK
    lane = lax.broadcasted_iota(jnp.int32, (8, 128), 1)
    row = jnp.concatenate([lens[...], jnp.zeros((1, 64), jnp.int32)], axis=1)
    row = jnp.broadcast_to(row, (8, 128))
    total = row
    for step in (1, 2, 4, 8, 16, 32):
        total = total + jnp.where(lane >= step, pltpu.roll(total, step, 1), 0)
    first = (total - row)[0:1, :] - start
    first = jnp.where(lane[0:1, :] < 64, first, 1 << 20)
    place = lax.broadcasted_iota(jnp.int32, (BLOCK, 128), 0)
    covered = jnp.where(first <= place, first, -(1 << 20))
    return jnp.max(covered.astype(F32), axis=1, keepdims=True).astype(jnp.int32)


def decay_rows(a):
    total = jnp.zeros((16, BLOCK), F32)
    for peer in range(PEERS):
        part = a[peer, DEC_ROW : DEC_ROW + 16, :]
        source = lax.broadcasted_iota(jnp.int32, (128, BLOCK), 0)
        place = lax.broadcasted_iota(jnp.int32, (128, BLOCK), 1)
        upto = jnp.where((source < TOK) & (source + peer * TOK <= place), 1.0, 0.0).astype(BF16)
        total = total + jnp.dot(part, upto, preferred_element_type=F32)
    return total


def gathered(a, index):
    return a[:, index * TOK : (index + 1) * TOK, :].reshape(BLOCK, HEAD)


def state(a, lens, out):
    begin = begins(lens)
    last = begin[BLOCK - 1 : BLOCK, :]
    rows = decay_rows(a)
    turned = jnp.transpose(rows)
    place = lax.broadcasted_iota(jnp.int32, (BLOCK, 1), 0)
    kept = place >= last
    extra = []
    for head in range(HEADS):
        sums = turned[:, head : head + 1]
        end = sums[BLOCK - 1 : BLOCK, :]
        weight = jnp.where(kept, jnp.exp(jnp.where(kept, sums - end, 0.0)), 0.0)
        key_map = silu(gathered(a, head).astype(F32)).astype(BF16).astype(F32)
        end_keys = (key_map * weight).astype(BF16)
        total = lax.dot_general(
            end_keys, gathered(a, 4 + head), (((0,), (0,)), ((), ())), preferred_element_type=F32
        )
        out[head * HEAD : (head + 1) * HEAD, :] = total.astype(BF16)
        extra.append(jnp.broadcast_to(jnp.where(last < 0, jnp.exp(-end), 0.0), (1, HEAD)))
    decay = jnp.concatenate([*extra, jnp.zeros((4, HEAD), F32)], axis=0)
    high = decay.astype(BF16).astype(F32)
    out[HEADS * HEAD :, :] = jnp.concatenate([high, decay - high], axis=0).astype(BF16)


def finish(a, b, near, far, lens, gain, lin_out, att_out, keys, values):
    begin = begins(lens)
    rows = decay_rows(a)
    turned = jnp.transpose(rows)
    shrink = near[HEADS * HEAD :, :].astype(F32)
    shrink = shrink[0:8, :] + shrink[8:16, :]
    for head in range(HEADS):
        query_map = silu(gathered(b, head).astype(F32)).astype(BF16)
        key_map = silu(gathered(a, head).astype(F32)).astype(BF16)
        value = gathered(a, 4 + head)
        piece = slice(head * HEAD, (head + 1) * HEAD)
        incoming = near[piece, :].astype(F32) + shrink[head : head + 1, :] * far[piece, :].astype(F32)
        carried = jnp.dot(query_map, incoming.astype(BF16), preferred_element_type=F32)
        sums = turned[:, head : head + 1]
        carried = carried * jnp.where(begin < 0, jnp.exp(-sums), 0.0)
        for tile in range(BLOCK // ROW_TILE):
            at = slice(tile * ROW_TILE, (tile + 1) * ROW_TILE)
            width = (tile + 1) * ROW_TILE
            scores = lax.dot_general(
                query_map[at], key_map[:width], (((1,), (1,)), ((), ())), preferred_element_type=F32
            )
            source = lax.broadcasted_iota(jnp.int32, (ROW_TILE, width), 1)
            place = lax.broadcasted_iota(jnp.int32, (ROW_TILE, width), 0) + tile * ROW_TILE
            allowed = (source <= place) & (source >= begin[at])
            gap = rows[head : head + 1, :width] - sums[at]
            weights = jnp.where(allowed, jnp.exp(jnp.where(allowed, gap, 0.0)), 0.0)
            inside = jnp.dot((weights * scores).astype(BF16), value[:width], preferred_element_type=F32)
            combined = inside + carried[at]
            mean = jnp.mean(combined * combined, axis=1, keepdims=True)
            normed = combined * lax.rsqrt(mean + 1e-6) * gain[:, piece]
            lin_out[at, piece] = normed.astype(BF16)

    for part, (ref, index) in enumerate(((b, 10), (b, 8), (a, 8))):
        keys[part * BLOCK : (part + 1) * BLOCK, :] = gathered(ref, index)
        values[part * BLOCK : (part + 1) * BLOCK, :] = gathered(ref, index + 1)
    for tile in range(BLOCK // ROW_TILE):
        at = slice(tile * ROW_TILE, (tile + 1) * ROW_TILE)
        near_keys = keys[tile * ROW_TILE : tile * ROW_TILE + SPAN, :]
        near_values = values[tile * ROW_TILE : tile * ROW_TILE + SPAN, :]
        source = lax.broadcasted_iota(jnp.int32, (ROW_TILE, SPAN), 1) - REACH
        place = lax.broadcasted_iota(jnp.int32, (ROW_TILE, SPAN), 0)
        allowed = (source <= place) & (source >= begin[at] - tile * ROW_TILE)
        for head in range(HEADS):
            query = b[2 * tile : 2 * tile + 2, (4 + head) * TOK : (5 + head) * TOK, :].reshape(ROW_TILE, HEAD)
            scores = lax.dot_general(
                query, near_keys, (((1,), (1,)), ((), ())), preferred_element_type=F32
            ) * (HEAD ** -0.5)
            scores = jnp.where(allowed, scores, -1e30)
            weights = jnp.exp(scores - jnp.max(scores, axis=1, keepdims=True))
            total = jnp.sum(weights, axis=1, keepdims=True)
            mixed = jnp.dot(weights.astype(BF16), near_values, preferred_element_type=F32)
            att_out[at, head * HEAD : (head + 1) * HEAD] = (mixed / total).astype(BF16)


def shifted(block, distance):
    count = lax.axis_size("ctx")
    return lax.ppermute(block, "ctx", [(i, i + distance) for i in range(count - distance)])


def exchanged(packed):
    return lax.all_to_all(packed, "uly", split_axis=0, concat_axis=0, tiled=True)


def shards(q, k, v, decay, gain, lens, aq, ak, av):
    lens = lens.reshape(1, 64)
    shape = lambda *dims: jax.ShapeDtypeStruct(dims, BF16)
    first, window = call(pack_first, (shape(PEERS, ROWS_A, HEAD), shape(PEERS, 2 * TOK, HEAD)))(k, v, ak, av, decay)
    a = exchanged(first)
    kv1, kv2 = shifted(window, 1), shifted(window, 2)
    second = call(pack_second, shape(PEERS, ROWS_B, HEAD))(q, aq, kv1, kv2)
    b = exchanged(second)
    own = call(state, shape(STATE_ROWS, HEAD))(a, lens)
    near, far = shifted(own, 1), shifted(own, 2)
    return call(
        finish,
        (shape(BLOCK, HEADS * HEAD), shape(BLOCK, HEADS * HEAD)),
        [pltpu.VMEM((3 * BLOCK, HEAD), BF16), pltpu.VMEM((3 * BLOCK, HEAD), BF16)],
    )(a, b, near, far, lens, gain.reshape(1, HEADS * HEAD))


def solution(mesh):
    rows = P(("ctx", "uly"), None)
    return jax.shard_map(
        shards,
        mesh=mesh,
        in_specs=(rows, rows, rows, rows, P("uly"), P(), rows, rows, rows),
        out_specs=(P("ctx", "uly"), P("ctx", "uly")),
        check_vma=False,
    )
```

```python
import math

import jax
import jax.numpy as jnp
from jax import lax
from jax.experimental import pallas as pl
from jax.experimental.pallas import tpu as pltpu
from jax.sharding import PartitionSpec as P

HEAD = 128
PEERS = 8
TOK = 64
HEADS = 4
BLOCK = PEERS * TOK
REACH = 2 * BLOCK
ROW_TILE = 128
LIN_TILE = 256
SPAN = REACH + ROW_TILE
DEC_ROW = 10 * TOK
ROWS_A = DEC_ROW + 16
ROWS_B = 10 * TOK
STATE_ROWS = HEADS * HEAD + 16
LOG2E = math.log2(math.e)
NEVER = -1e30
F32 = jnp.float32
BF16 = jnp.bfloat16
VMEM_LIMIT = 40 * 1024 * 1024


def silu(x):
    half = 0.5 * x.astype(F32)
    return (half + half * jnp.tanh(half)).astype(BF16)


def near_core(x):
    return pltpu.with_memory_space_constraint(x, pltpu.VMEM)


def call(body, out_shape, scratch=(), inputs=None):
    whole = pl.BlockSpec(memory_space=pltpu.VMEM)
    many = isinstance(out_shape, (tuple, list))
    return pl.pallas_call(
        body,
        out_shape=out_shape,
        **({} if inputs is None else dict(in_specs=inputs)),
        out_specs=tuple(whole for _ in out_shape) if many else whole,
        scratch_shapes=list(scratch),
        compiler_params=pltpu.CompilerParams(vmem_limit_bytes=VMEM_LIMIT),
    )


def columns(out, source, first, count):
    for peer in range(PEERS):
        for i in range(count):
            column = (peer * count + i) * HEAD
            out[peer, (first + i) * TOK : (first + i + 1) * TOK, :] = source[:, column : column + HEAD]


def pack_first(k, v, ak, av, decay, out, window, k_in, v_in, ak_in, av_in, decay_in, arrived):
    pairs = ((ak, ak_in), (av, av_in), (decay, decay_in), (k, k_in), (v, v_in))
    copies = [pltpu.make_async_copy(source, into, arrived.at[i]) for i, (source, into) in enumerate(pairs)]
    for copy in copies:
        copy.start()
    copies[0].wait()
    columns(out, ak_in, 8, 1)
    columns(window, ak_in, 0, 1)
    copies[1].wait()
    columns(out, av_in, 9, 1)
    columns(window, av_in, 1, 1)
    copies[2].wait()
    rows = jnp.concatenate([decay_in[...].astype(F32), jnp.zeros((32, 64), F32)], axis=1)
    for peer in range(PEERS):
        own = rows[HEADS * peer : HEADS * (peer + 1), :]
        own = jnp.concatenate([own, own, jnp.zeros((8, 128), F32)], axis=0)
        out[peer, DEC_ROW : DEC_ROW + 16, :] = own.astype(BF16)
    copies[3].wait()
    columns(out, k_in, 0, HEADS)
    copies[4].wait()
    columns(out, v_in, 4, HEADS)


def pack_second(q, aq, earlier, out):
    columns(out, aq, 4, HEADS)
    columns(out, q, 0, HEADS)
    out[:, 8 * TOK :, :] = earlier[...]


def begins(lens):
    start = lax.axis_index("ctx") * BLOCK
    lane = lax.broadcasted_iota(jnp.int32, (8, 128), 1)
    row = jnp.concatenate([lens[...], jnp.zeros((1, 64), jnp.int32)], axis=1)
    row = jnp.broadcast_to(row, (8, 128))
    total = row
    for step in (1, 2, 4, 8, 16, 32):
        total = total + jnp.where(lane >= step, pltpu.roll(total, step, 1), 0)
    first = (total - row)[0:1, :] - start
    first = jnp.where(lane[0:1, :] < 64, first, 1 << 20).astype(F32)
    place = lax.broadcasted_iota(jnp.int32, (BLOCK, 128), 0).astype(F32)
    return jnp.max(jnp.where(first <= place, first, -float(1 << 20)), axis=1, keepdims=True)


def decay_rows(a):
    source = lax.broadcasted_iota(jnp.int32, (128, 128), 0)
    place = lax.broadcasted_iota(jnp.int32, (128, 128), 1)
    low = jnp.where((source < TOK) & (source <= place), 1.0, 0.0).astype(BF16)
    high = jnp.where((source < TOK) & (source + TOK <= place), 1.0, 0.0).astype(BF16)
    before = jnp.zeros((16, 1), F32)
    parts = []
    for pair in range(PEERS // 2):
        part = jnp.dot(a[2 * pair, DEC_ROW : DEC_ROW + 16, :], low, preferred_element_type=F32)
        part += jnp.dot(a[2 * pair + 1, DEC_ROW : DEC_ROW + 16, :], high, preferred_element_type=F32)
        part += before
        before = part[:, 127:128]
        parts.append(part)
    return jnp.concatenate(parts, axis=1) * LOG2E


def gathered(a, index):
    return a[:, index * TOK : (index + 1) * TOK, :].reshape(BLOCK, HEAD)


def state(a, lens, out, all_out, cols, rows, maps):
    for index in range(2):
        all_out[STATE_ROWS + index * BLOCK : STATE_ROWS + (index + 1) * BLOCK, :] = gathered(a, 8 + index)
    begin = begins(lens)
    sums = decay_rows(a)
    rows[...] = sums
    turned = jnp.transpose(jnp.concatenate([sums, jnp.zeros((112, BLOCK), F32)], axis=0))
    lane = lax.broadcasted_iota(jnp.int32, (BLOCK, HEAD), 1)
    carry = jnp.where(begin < 0, jnp.exp2(-turned), 0.0)
    cols[...] = jnp.where(lane < HEADS, turned, jnp.where(lane == 8, begin, carry))
    last = begin[BLOCK - 1 : BLOCK, :]
    end = turned[BLOCK - 1 : BLOCK, :]
    place = lax.broadcasted_iota(jnp.int32, (BLOCK, 1), 0).astype(F32)
    weight = jnp.exp2(jnp.where(place >= last, turned - end, NEVER))
    extra = []
    for head in range(HEADS):
        key_map = silu(gathered(a, head))
        maps[head * BLOCK : (head + 1) * BLOCK, :] = key_map
        end_keys = (key_map.astype(F32) * weight[:, head : head + 1]).astype(BF16)
        total = lax.dot_general(
            end_keys, gathered(a, 4 + head), (((0,), (0,)), ((), ())), preferred_element_type=F32
        )
        out[head * HEAD : (head + 1) * HEAD, :] = total.astype(BF16)
        all_out[head * HEAD : (head + 1) * HEAD, :] = total.astype(BF16)
        gone = jnp.where(last < 0, jnp.exp2(-end[:, head : head + 1]), 0.0)
        extra.append(jnp.broadcast_to(gone, (1, HEAD)))
    decay = jnp.concatenate([*extra, jnp.zeros((4, HEAD), F32)], axis=0)
    high = decay.astype(BF16).astype(F32)
    parts = jnp.concatenate([high, decay - high], axis=0).astype(BF16)
    out[HEADS * HEAD :, :] = parts
    all_out[HEADS * HEAD : STATE_ROWS, :] = parts


def attention(a, b, near, cols, att_out, keys, values, bias):
    values[:, HEAD:] = jnp.ones((3 * BLOCK, HEAD), BF16)
    for index, ref in enumerate((keys, values)):
        ref[:BLOCK, :HEAD] = gathered(b, 8 + index)
        ref[BLOCK : 2 * BLOCK, :HEAD] = near[STATE_ROWS + index * BLOCK : STATE_ROWS + (index + 1) * BLOCK, :]
        ref[2 * BLOCK :, :HEAD] = gathered(a, 8 + index)
    source = (lax.broadcasted_iota(jnp.int32, (ROW_TILE, SPAN), 1) - REACH).astype(F32)
    place = lax.broadcasted_iota(jnp.int32, (ROW_TILE, SPAN), 0).astype(F32)
    for tile in range(BLOCK // ROW_TILE):
        at = slice(tile * ROW_TILE, (tile + 1) * ROW_TILE)
        span = slice(tile * ROW_TILE, tile * ROW_TILE + SPAN)
        begin = cols[at, 8:9] - float(tile * ROW_TILE)
        bias[...] = jnp.where((source <= place) & (source >= begin), 0.0, NEVER)
        for head in range(HEADS):
            query = b[2 * tile : 2 * tile + 2, (4 + head) * TOK : (5 + head) * TOK, :].reshape(ROW_TILE, HEAD)
            scores = lax.dot_general(
                query, keys[span, :], (((1,), (1,)), ((), ())), preferred_element_type=F32
            )
            scores = scores * (HEAD ** -0.5 * LOG2E) + bias[...]
            weights = jnp.exp2(scores - jnp.max(scores, axis=1, keepdims=True)).astype(BF16)
            mixed = jnp.dot(weights, values[span, :], preferred_element_type=F32)
            att_out[at, head * HEAD : (head + 1) * HEAD] = (mixed[:, :HEAD] / mixed[:, HEAD:]).astype(BF16)


def lightning(a, b, near, far, cols, rows, maps, gain, lin_out, queries, incoming):
    shrink = near[HEADS * HEAD : STATE_ROWS, :].astype(F32)
    shrink = shrink[0:8, :] + shrink[8:16, :]
    pieces = [slice(head * HEAD, (head + 1) * HEAD) for head in range(HEADS)]
    for head, piece in enumerate(pieces):
        queries[head * BLOCK : (head + 1) * BLOCK, :] = silu(gathered(b, head))
        both = near[piece, :].astype(F32) + shrink[head : head + 1, :] * far[piece, :].astype(F32)
        incoming[piece, :] = both.astype(BF16)
    for tile in range(BLOCK // LIN_TILE):
        at = slice(tile * LIN_TILE, (tile + 1) * LIN_TILE)
        width = (tile + 1) * LIN_TILE
        peers = width // TOK
        source = lax.broadcasted_iota(jnp.int32, (LIN_TILE, width), 1).astype(F32)
        place = lax.broadcasted_iota(jnp.int32, (LIN_TILE, width), 0).astype(F32) + float(tile * LIN_TILE)
        bias = jnp.where((source <= place) & (source >= cols[at, 8:9]), 0.0, NEVER)
        query = [queries[head * BLOCK + tile * LIN_TILE : head * BLOCK + width, :] for head in range(HEADS)]
        carried = [jnp.dot(query[h], incoming[pieces[h], :], preferred_element_type=F32) for h in range(HEADS)]
        scores = [
            lax.dot_general(
                query[h],
                maps[h * BLOCK : h * BLOCK + width, :],
                (((1,), (1,)), ((), ())),
                preferred_element_type=F32,
            )
            for h in range(HEADS)
        ]
        gaps = [(rows[h : h + 1, :width] - cols[at, h : h + 1]) + bias for h in range(HEADS)]
        weighted = [(jnp.exp2(gaps[h]) * scores[h]).astype(BF16) for h in range(HEADS)]
        inside = [
            jnp.dot(
                weighted[h],
                a[:peers, (4 + h) * TOK : (5 + h) * TOK, :].reshape(width, HEAD),
                preferred_element_type=F32,
            )
            for h in range(HEADS)
        ]
        for h, piece in enumerate(pieces):
            combined = inside[h] + carried[h] * cols[at, 4 + h : 5 + h]
            mean = jnp.mean(combined * combined, axis=1, keepdims=True)
            lin_out[at, piece] = (combined * lax.rsqrt(mean + 1e-6) * gain[:, piece]).astype(BF16)


def shifted(block, distance):
    count = lax.axis_size("ctx")
    return lax.ppermute(block, "ctx", [(i, i + distance) for i in range(count - distance)])


def exchanged(packed):
    return lax.all_to_all(packed, "uly", split_axis=0, concat_axis=0, tiled=True)


def shards(q, k, v, decay, gain, lens, aq, ak, av):
    lens = lens.reshape(1, 64)
    fast = lambda dtype, *dims: pltpu.VMEM(dims, dtype)
    shape = lambda *dims: jax.ShapeDtypeStruct(dims, BF16)
    first, window = call(
        pack_first,
        (fast(BF16, PEERS, ROWS_A, HEAD), fast(BF16, PEERS, 2 * TOK, HEAD)),
        [
            pltpu.VMEM((TOK, PEERS * HEADS * HEAD), BF16),
            pltpu.VMEM((TOK, PEERS * HEADS * HEAD), BF16),
            pltpu.VMEM((TOK, PEERS * HEAD), BF16),
            pltpu.VMEM((TOK, PEERS * HEAD), BF16),
            pltpu.VMEM((PEERS * HEADS, TOK), BF16),
            pltpu.SemaphoreType.DMA((5,)),
        ],
        [pl.BlockSpec(memory_space=pltpu.HBM)] * 5,
    )(*(pltpu.with_memory_space_constraint(x, pltpu.HBM) for x in (k, v, ak, av, decay.T)))
    a = near_core(exchanged(first))
    earlier = shifted(window, 2)
    b = near_core(exchanged(call(pack_second, fast(BF16, PEERS, ROWS_B, HEAD))(q, aq, near_core(earlier))))
    own, all_own, cols, rows, maps = call(
        state,
        (
            fast(BF16, STATE_ROWS, HEAD),
            fast(BF16, STATE_ROWS + 2 * BLOCK, HEAD),
            fast(F32, BLOCK, HEAD),
            fast(F32, 16, BLOCK),
            fast(BF16, HEADS * BLOCK, HEAD),
        ),
    )(a, lens)
    near, far = shifted(all_own, 1), shifted(own, 2)
    att_out = call(
        attention,
        shape(BLOCK, HEADS * HEAD),
        [
            pltpu.VMEM((3 * BLOCK, HEAD), BF16),
            pltpu.VMEM((3 * BLOCK, 2 * HEAD), BF16),
            pltpu.VMEM((ROW_TILE, SPAN), F32),
        ],
    )(a, b, near_core(near), near_core(cols))
    lin_out = call(
        lightning,
        shape(BLOCK, HEADS * HEAD),
        [pltpu.VMEM((HEADS * BLOCK, HEAD), BF16), pltpu.VMEM((HEADS * HEAD, HEAD), BF16)],
    )(
        a,
        b,
        near_core(near),
        near_core(far),
        near_core(cols),
        near_core(rows),
        near_core(maps),
        gain.reshape(1, HEADS * HEAD),
    )
    return lin_out, att_out


def solution(mesh):
    rows = P(("ctx", "uly"), None)
    return jax.shard_map(
        shards,
        mesh=mesh,
        in_specs=(rows, rows, rows, rows, P("uly"), P(), rows, rows, rows),
        out_specs=(P("ctx", "uly"), P("ctx", "uly")),
        check_vma=False,
    )
```

```python
import math

import jax
import jax.numpy as jnp
from jax import lax
from jax.experimental import pallas as pl
from jax.experimental.pallas import tpu as pltpu
from jax.sharding import PartitionSpec as P

HEAD = 128
PEERS = 8
TOK = 64
HEADS = 4
BLOCK = PEERS * TOK
REACH = 2 * BLOCK
ROW_TILE = 128
LIN_TILE = 256
PART = BLOCK + ROW_TILE
DEC_ROW = 10 * TOK
ROWS_A = DEC_ROW + 16
ROWS_B = 10 * TOK
STATE_ROWS = HEADS * HEAD + 16
LOG2E = math.log2(math.e)
NEVER = -1e30
SCALE = HEAD ** -0.5 * LOG2E
F32 = jnp.float32
BF16 = jnp.bfloat16
VMEM_LIMIT = 24 * 1024 * 1024


def silu(x):
    half = 0.5 * x.astype(F32)
    return (half + half * jnp.tanh(half)).astype(BF16)


def near_core(x):
    return pltpu.with_memory_space_constraint(x, pltpu.VMEM)


def call(body, out_shape, scratch=(), inputs=None, output=pl.BlockSpec(memory_space=pltpu.VMEM)):
    many = isinstance(out_shape, (tuple, list))
    return pl.pallas_call(
        body,
        out_shape=out_shape,
        **({} if inputs is None else dict(in_specs=inputs)),
        out_specs=tuple(output for _ in out_shape) if many else output,
        scratch_shapes=list(scratch),
        compiler_params=pltpu.CompilerParams(vmem_limit_bytes=VMEM_LIMIT),
    )


def columns(out, source, first, count):
    for peer in range(PEERS):
        for i in range(count):
            column = (peer * count + i) * HEAD
            out[peer, (first + i) * TOK : (first + i + 1) * TOK, :] = source[:, column : column + HEAD]


def pack_first(k, v, ak, av, decay, out, window, k_in, v_in, ak_in, av_in, decay_in, staged, raw, arrived, left):
    pairs = ((ak, ak_in), (av, av_in), (decay, decay_in), (k, k_in), (v, v_in))
    copies = [pltpu.make_async_copy(source, into, arrived.at[i]) for i, (source, into) in enumerate(pairs)]
    for copy in copies:
        copy.start()
    parts = [slice(8 * TOK, ROWS_A), slice(0, 4 * TOK), slice(4 * TOK, 8 * TOK)]
    away = [pltpu.make_async_copy(staged.at[:, part], out.at[:, part], left.at[i]) for i, part in enumerate(parts)]
    away.append(pltpu.make_async_copy(raw, window, left.at[3]))
    copies[0].wait()
    columns(staged, ak_in, 8, 1)
    columns(raw, ak_in, 0, 1)
    copies[1].wait()
    columns(staged, av_in, 9, 1)
    columns(raw, av_in, 1, 1)
    copies[2].wait()
    rows = jnp.concatenate([decay_in[...].astype(F32), jnp.zeros((32, 64), F32)], axis=1)
    for peer in range(PEERS):
        own = rows[HEADS * peer : HEADS * (peer + 1), :]
        own = jnp.concatenate([own, own, jnp.zeros((8, 128), F32)], axis=0)
        staged[peer, DEC_ROW : DEC_ROW + 16, :] = own.astype(BF16)
    away[0].start()
    away[3].start()
    copies[3].wait()
    columns(staged, k_in, 0, HEADS)
    away[1].start()
    copies[4].wait()
    columns(staged, v_in, 4, HEADS)
    away[2].start()
    for copy in away:
        copy.wait()


def pack_second(q, aq, out):
    columns(out, aq, 4, HEADS)
    columns(out, q, 0, HEADS)


def pack_body(q, aq, out, staged, done):
    pack_second(q, aq, staged)
    copy = pltpu.make_async_copy(staged, out.at[:, : 8 * TOK, :], done)
    copy.start()
    copy.wait()


def insert(earlier, packed, out, done):
    copy = pltpu.make_async_copy(earlier, out.at[:, 8 * TOK :, :], done)
    copy.start()
    copy.wait()


def begins(lens):
    start = lax.axis_index("ctx") * BLOCK
    lane = lax.broadcasted_iota(jnp.int32, (8, 128), 1)
    row = jnp.concatenate([lens[...], jnp.zeros((1, 64), jnp.int32)], axis=1)
    row = jnp.broadcast_to(row, (8, 128))
    total = row
    for step in (1, 2, 4, 8, 16, 32):
        total = total + jnp.where(lane >= step, pltpu.roll(total, step, 1), 0)
    first = (total - row)[0:1, :] - start
    first = jnp.where(lane[0:1, :] < 64, first, 1 << 20).astype(F32)
    place = lax.broadcasted_iota(jnp.int32, (BLOCK, 128), 0).astype(F32)
    return jnp.max(jnp.where(first <= place, first, -float(1 << 20)), axis=1, keepdims=True)


def decay_rows(a):
    source = lax.broadcasted_iota(jnp.int32, (128, 128), 0)
    place = lax.broadcasted_iota(jnp.int32, (128, 128), 1)
    low = jnp.where((source < TOK) & (source <= place), 1.0, 0.0).astype(BF16)
    high = jnp.where((source < TOK) & (source + TOK <= place), 1.0, 0.0).astype(BF16)
    before = jnp.zeros((16, 1), F32)
    parts = []
    for pair in range(PEERS // 2):
        part = jnp.dot(a[2 * pair, DEC_ROW : DEC_ROW + 16, :], low, preferred_element_type=F32)
        part += jnp.dot(a[2 * pair + 1, DEC_ROW : DEC_ROW + 16, :], high, preferred_element_type=F32)
        part += before
        before = part[:, 127:128]
        parts.append(part)
    return jnp.concatenate(parts, axis=1) * LOG2E


def gathered(a, index):
    return a[:, index * TOK : (index + 1) * TOK, :].reshape(BLOCK, HEAD)


def state(a, lens, out, all_out, cols, rows):
    for index in range(2):
        all_out[STATE_ROWS + index * BLOCK : STATE_ROWS + (index + 1) * BLOCK, :] = gathered(a, 8 + index)
    begin = begins(lens)
    sums = decay_rows(a)
    rows[...] = sums
    turned = jnp.transpose(jnp.concatenate([sums, jnp.zeros((112, BLOCK), F32)], axis=0))
    lane = lax.broadcasted_iota(jnp.int32, (BLOCK, HEAD), 1)
    carry = jnp.where(begin < 0, jnp.exp2(-turned), 0.0)
    cols[...] = jnp.where(lane < HEADS, turned, jnp.where(lane == 8, begin, carry))
    last = begin[BLOCK - 1 : BLOCK, :]
    end = turned[BLOCK - 1 : BLOCK, :]
    place = lax.broadcasted_iota(jnp.int32, (BLOCK, 1), 0).astype(F32)
    weight = jnp.exp2(jnp.where(place >= last, turned - end, NEVER))
    extra = []
    for head in range(HEADS):
        key_map = silu(gathered(a, head))
        end_keys = (key_map.astype(F32) * weight[:, head : head + 1]).astype(BF16)
        total = lax.dot_general(
            end_keys, gathered(a, 4 + head), (((0,), (0,)), ((), ())), preferred_element_type=F32
        )
        out[head * HEAD : (head + 1) * HEAD, :] = total.astype(BF16)
        all_out[head * HEAD : (head + 1) * HEAD, :] = total.astype(BF16)
        gone = jnp.where(last < 0, jnp.exp2(-end[:, head : head + 1]), 0.0)
        extra.append(jnp.broadcast_to(gone, (1, HEAD)))
    decay = jnp.concatenate([*extra, jnp.zeros((4, HEAD), F32)], axis=0)
    high = decay.astype(BF16).astype(F32)
    parts = jnp.concatenate([high, decay - high], axis=0).astype(BF16)
    out[HEADS * HEAD :, :] = parts
    all_out[HEADS * HEAD : STATE_ROWS, :] = parts


def within(a, b, cols, rows, mixed_out, highest_out, inside_out, queries, keys, values, bias, maps):
    values[:, HEAD:] = jnp.ones((2 * BLOCK, HEAD), BF16)
    for index, ref in enumerate((keys, values)):
        ref[:BLOCK, :HEAD] = gathered(b, 8 + index)
        ref[BLOCK:, :HEAD] = gathered(a, 8 + index)
    lane = lax.broadcasted_iota(jnp.int32, (ROW_TILE, PART), 1)
    place = lax.broadcasted_iota(jnp.int32, (ROW_TILE, PART), 0).astype(F32)
    for tile in range(BLOCK // ROW_TILE):
        at = slice(tile * ROW_TILE, (tile + 1) * ROW_TILE)
        span = slice(tile * ROW_TILE, tile * ROW_TILE + PART)
        begin = cols[at, 8:9] - float(tile * ROW_TILE)
        source = jnp.where(lane < BLOCK - tile * ROW_TILE, lane - REACH, lane - BLOCK).astype(F32)
        bias[...] = jnp.where((source <= place) & (source >= begin), 0.0, NEVER)
        for head in range(HEADS):
            query = b[2 * tile : 2 * tile + 2, (4 + head) * TOK : (5 + head) * TOK, :].reshape(ROW_TILE, HEAD)
            scores = lax.dot_general(
                query, keys[span, :], (((1,), (1,)), ((), ())), preferred_element_type=F32
            )
            scores = scores * SCALE + bias[...]
            highest = jnp.max(scores, axis=1, keepdims=True)
            weights = jnp.exp2(scores - highest).astype(BF16)
            mixed_out[at, 2 * head * HEAD : 2 * (head + 1) * HEAD] = jnp.dot(
                weights, values[span, :], preferred_element_type=F32
            )
            highest_out[at, head * HEAD : (head + 1) * HEAD] = jnp.broadcast_to(highest, (ROW_TILE, HEAD))

    for head in range(HEADS):
        queries[head * BLOCK : (head + 1) * BLOCK, :] = silu(gathered(b, head))
        maps[head * BLOCK : (head + 1) * BLOCK, :] = silu(gathered(a, head))
    for tile in range(BLOCK // LIN_TILE):
        at = slice(tile * LIN_TILE, (tile + 1) * LIN_TILE)
        width = (tile + 1) * LIN_TILE
        peers = width // TOK
        source = lax.broadcasted_iota(jnp.int32, (LIN_TILE, width), 1).astype(F32)
        place = lax.broadcasted_iota(jnp.int32, (LIN_TILE, width), 0).astype(F32) + float(tile * LIN_TILE)
        allowed = jnp.where((source <= place) & (source >= cols[at, 8:9]), 0.0, NEVER)
        scores = [
            lax.dot_general(
                queries[h * BLOCK + tile * LIN_TILE : h * BLOCK + width, :],
                maps[h * BLOCK : h * BLOCK + width, :],
                (((1,), (1,)), ((), ())),
                preferred_element_type=F32,
            )
            for h in range(HEADS)
        ]
        gaps = [(rows[h : h + 1, :width] - cols[at, h : h + 1]) + allowed for h in range(HEADS)]
        weighted = [(jnp.exp2(gaps[h]) * scores[h]).astype(BF16) for h in range(HEADS)]
        for h in range(HEADS):
            inside_out[at, h * HEAD : (h + 1) * HEAD] = jnp.dot(
                weighted[h],
                a[:peers, (4 + h) * TOK : (5 + h) * TOK, :].reshape(width, HEAD),
                preferred_element_type=F32,
            )


def finish(b, near, far, cols, mixed_in, highest_in, inside, queries, gain, lin_out, att_out, values, att, lin, done):
    values[:, HEAD:] = jnp.ones((BLOCK, HEAD), BF16)
    values[:, :HEAD] = near[STATE_ROWS + BLOCK :, :]
    seen = (lax.broadcasted_iota(jnp.int32, (ROW_TILE, BLOCK), 1) - BLOCK).astype(F32)
    tiles = [slice(tile * ROW_TILE, (tile + 1) * ROW_TILE) for tile in range(BLOCK // ROW_TILE)]
    pieces = [slice(head * HEAD, (head + 1) * HEAD) for head in range(HEADS)]
    copies = []
    for tile, at in enumerate(tiles):
        allowed = jnp.where(seen >= cols[at, 8:9], 0.0, NEVER)
        for head, piece in enumerate(pieces):
            query = b[2 * tile : 2 * tile + 2, (4 + head) * TOK : (5 + head) * TOK, :].reshape(ROW_TILE, HEAD)
            scores = lax.dot_general(
                query,
                near[STATE_ROWS : STATE_ROWS + BLOCK, :],
                (((1,), (1,)), ((), ())),
                preferred_element_type=F32,
            )
            scores = scores * SCALE + allowed
            before = highest_in[at, piece]
            highest = jnp.maximum(jnp.max(scores, axis=1, keepdims=True), before)
            weights = [jnp.exp2(scores[:, c : c + HEAD] - highest).astype(BF16) for c in range(0, BLOCK, HEAD)]
            shrink = jnp.exp2(before - highest)
            mixed = jnp.dot(jnp.concatenate(weights, axis=1), values[...], preferred_element_type=F32)
            first = 2 * head * HEAD
            top = mixed[:, :HEAD] + shrink * mixed_in[at, first : first + HEAD]
            total = mixed[:, HEAD:] + shrink * mixed_in[at, first + HEAD : first + 2 * HEAD]
            att[at, piece] = (top / total).astype(BF16)
        copies.append(pltpu.make_async_copy(att.at[at], att_out.at[at], done.at[tile]))
        copies[-1].start()
    shrink = near[HEADS * HEAD : STATE_ROWS, :].astype(F32)
    shrink = shrink[0:8, :] + shrink[8:16, :]
    incoming = [
        (near[piece, :].astype(F32) + shrink[head : head + 1, :] * far[piece, :].astype(F32)).astype(BF16)
        for head, piece in enumerate(pieces)
    ]
    for tile, at in enumerate(tiles):
        carried = [
            jnp.dot(
                queries[head * BLOCK + tile * ROW_TILE : head * BLOCK + (tile + 1) * ROW_TILE, :],
                incoming[head],
                preferred_element_type=F32,
            )
            for head in range(HEADS)
        ]
        for head, piece in enumerate(pieces):
            combined = inside[at, piece] + carried[head] * cols[at, 4 + head : 5 + head]
            mean = jnp.mean(combined * combined, axis=1, keepdims=True)
            lin[at, piece] = (combined * lax.rsqrt(mean + 1e-6) * gain[:, piece]).astype(BF16)
        copies.append(pltpu.make_async_copy(lin.at[at], lin_out.at[at], done.at[len(tiles) + tile]))
        copies[-1].start()
    for copy in copies:
        copy.wait()


def shifted(block, distance):
    count = lax.axis_size("ctx")
    return lax.ppermute(block, "ctx", [(i, i + distance) for i in range(count - distance)])


def exchanged(packed):
    return lax.all_to_all(packed, "uly", split_axis=0, concat_axis=0, tiled=True)


def shards(q, k, v, decay, gain, lens, aq, ak, av):
    lens = lens.reshape(1, 64)
    fast = lambda dtype, *dims: pltpu.VMEM(dims, dtype)
    shape = lambda *dims: jax.ShapeDtypeStruct(dims, BF16)
    wide, narrow = PEERS * HEADS * HEAD, PEERS * HEAD
    far_core = lambda x: pltpu.with_memory_space_constraint(x, pltpu.HBM)
    in_hbm = pl.BlockSpec(memory_space=pltpu.HBM)
    first, window = call(
        pack_first,
        (shape(PEERS, ROWS_A, HEAD), shape(PEERS, 2 * TOK, HEAD)),
        [
            pltpu.VMEM((TOK, wide), BF16),
            pltpu.VMEM((TOK, wide), BF16),
            pltpu.VMEM((TOK, narrow), BF16),
            pltpu.VMEM((TOK, narrow), BF16),
            pltpu.VMEM((PEERS * HEADS, TOK), BF16),
            pltpu.VMEM((PEERS, ROWS_A, HEAD), BF16),
            pltpu.VMEM((PEERS, 2 * TOK, HEAD), BF16),
            pltpu.SemaphoreType.DMA((5,)),
            pltpu.SemaphoreType.DMA((4,)),
        ],
        [in_hbm] * 5,
        in_hbm,
    )(*(far_core(x) for x in (k, v, ak, av, decay.T)))
    a = near_core(exchanged(first))
    earlier = shifted(window, 2)
    second = call(
        pack_body, pltpu.HBM((PEERS, ROWS_B, HEAD), BF16),
        [pltpu.VMEM((PEERS, 8 * TOK, HEAD), BF16), pltpu.SemaphoreType.DMA], output=in_hbm,
    )(q, aq)
    second = pl.pallas_call(
        insert,
        out_shape=pltpu.HBM((PEERS, ROWS_B, HEAD), BF16),
        in_specs=[pl.BlockSpec(memory_space=pltpu.VMEM), in_hbm],
        out_specs=in_hbm,
        input_output_aliases={1: 0},
        scratch_shapes=[pltpu.SemaphoreType.DMA],
    )(near_core(earlier), far_core(second))
    b = near_core(exchanged(second))
    own, all_own, cols, rows = call(
        state,
        (
            fast(BF16, STATE_ROWS, HEAD),
            fast(BF16, STATE_ROWS + 2 * BLOCK, HEAD),
            fast(F32, BLOCK, HEAD),
            fast(F32, 16, BLOCK),
        ),
    )(a, lens)
    near, far = near_core(shifted(all_own, 1)), near_core(shifted(own, 2))
    cols, rows = near_core(cols), near_core(rows)
    mixed, highest, inside, queries = call(
        within,
        (
            fast(F32, BLOCK, 2 * HEADS * HEAD),
            fast(F32, BLOCK, HEADS * HEAD),
            fast(F32, BLOCK, HEADS * HEAD),
            fast(BF16, HEADS * BLOCK, HEAD),
        ),
        [
            pltpu.VMEM((2 * BLOCK, HEAD), BF16),
            pltpu.VMEM((2 * BLOCK, 2 * HEAD), BF16),
            pltpu.VMEM((ROW_TILE, PART), F32),
            pltpu.VMEM((HEADS * BLOCK, HEAD), BF16),
        ],
    )(a, b, cols, rows)
    lin_out, att_out = call(
        finish,
        (shape(BLOCK, HEADS * HEAD), shape(BLOCK, HEADS * HEAD)),
        [
            pltpu.VMEM((BLOCK, 2 * HEAD), BF16),
            pltpu.VMEM((BLOCK, HEADS * HEAD), BF16),
            pltpu.VMEM((BLOCK, HEADS * HEAD), BF16),
            pltpu.SemaphoreType.DMA((2 * BLOCK // ROW_TILE,)),
        ],
        output=in_hbm,
    )(
        b,
        near,
        far,
        cols,
        near_core(mixed),
        near_core(highest),
        near_core(inside),
        near_core(queries),
        gain.reshape(1, HEADS * HEAD),
    )
    return lin_out, att_out


def solution(mesh):
    rows = P(("ctx", "uly"), None)
    return jax.shard_map(
        shards,
        mesh=mesh,
        in_specs=(rows, rows, rows, rows, P("uly"), P(), rows, rows, rows),
        out_specs=(P("ctx", "uly"), P("ctx", "uly")),
        check_vma=False,
    )
```

```python
import math

import jax
import jax.numpy as jnp
from jax import lax
from jax.experimental import pallas as pl
from jax.experimental.pallas import tpu as pltpu
from jax.sharding import PartitionSpec as P

HEAD = 128
PEERS = 8
TOK = 64
HEADS = 4
BLOCK = PEERS * TOK
REACH = 2 * BLOCK
ROW_TILE = 128
LIN_TILE = 256
PART = BLOCK + ROW_TILE
DEC_ROW = 10 * TOK
ROWS_A = DEC_ROW + 16
ROWS_B = 10 * TOK
STATE_ROWS = HEADS * HEAD + 16
LOG2E = math.log2(math.e)
NEVER = -1e30
SCALE = HEAD ** -0.5 * LOG2E
F32 = jnp.float32
BF16 = jnp.bfloat16
VMEM_LIMIT = 24 * 1024 * 1024


def silu(x):
    half = 0.5 * x.astype(F32)
    return (half + half * jnp.tanh(half)).astype(BF16)


def near_core(x):
    return pltpu.with_memory_space_constraint(x, pltpu.VMEM)


def call(body, out_shape, scratch=(), inputs=None, output=pl.BlockSpec(memory_space=pltpu.VMEM)):
    many = isinstance(out_shape, (tuple, list))
    return pl.pallas_call(
        body,
        out_shape=out_shape,
        **({} if inputs is None else dict(in_specs=inputs)),
        out_specs=tuple(output for _ in out_shape) if many else output,
        scratch_shapes=list(scratch),
        compiler_params=pltpu.CompilerParams(vmem_limit_bytes=VMEM_LIMIT),
    )


def columns(out, source, first, count):
    for peer in range(PEERS):
        for i in range(count):
            column = (peer * count + i) * HEAD
            out[peer, (first + i) * TOK : (first + i + 1) * TOK, :] = source[:, column : column + HEAD]


def pack_first(k, v, ak, av, decay, out, window, k_in, v_in, ak_in, av_in, decay_in, staged, raw, arrived, left):
    pairs = ((ak, ak_in), (av, av_in), (decay, decay_in), (k, k_in), (v, v_in))
    copies = [pltpu.make_async_copy(source, into, arrived.at[i]) for i, (source, into) in enumerate(pairs)]
    for copy in copies:
        copy.start()
    parts = [slice(8 * TOK, ROWS_A), slice(0, 4 * TOK), slice(4 * TOK, 8 * TOK)]
    away = [pltpu.make_async_copy(staged.at[:, part], out.at[:, part], left.at[i]) for i, part in enumerate(parts)]
    away.append(pltpu.make_async_copy(raw, window, left.at[3]))
    copies[0].wait()
    columns(staged, ak_in, 8, 1)
    columns(raw, ak_in, 0, 1)
    copies[1].wait()
    columns(staged, av_in, 9, 1)
    columns(raw, av_in, 1, 1)
    copies[2].wait()
    rows = jnp.concatenate([decay_in[...].astype(F32), jnp.zeros((32, 64), F32)], axis=1)
    for peer in range(PEERS):
        own = rows[HEADS * peer : HEADS * (peer + 1), :]
        own = jnp.concatenate([own, own, jnp.zeros((8, 128), F32)], axis=0)
        staged[peer, DEC_ROW : DEC_ROW + 16, :] = own.astype(BF16)
    away[0].start()
    away[3].start()
    copies[3].wait()
    columns(staged, k_in, 0, HEADS)
    away[1].start()
    copies[4].wait()
    columns(staged, v_in, 4, HEADS)
    away[2].start()
    for copy in away:
        copy.wait()


def pack_second(q, aq, out):
    columns(out, aq, 4, HEADS)
    columns(out, q, 0, HEADS)


def pack_body(q, aq, out, staged, done):
    pack_second(q, aq, staged)
    copy = pltpu.make_async_copy(staged, out.at[:, : 8 * TOK, :], done)
    copy.start()
    copy.wait()


def insert(earlier, packed, out, done):
    copy = pltpu.make_async_copy(earlier, out.at[:, 8 * TOK :, :], done)
    copy.start()
    copy.wait()


def starts(lens):
    start = lax.axis_index("ctx") * BLOCK
    lane = lax.broadcasted_iota(jnp.int32, (8, 128), 1)
    row = jnp.concatenate([lens[...], jnp.zeros((1, 64), jnp.int32)], axis=1)
    row = jnp.broadcast_to(row, (8, 128))
    total = row
    for step in (1, 2, 4, 8, 16, 32):
        total = total + jnp.where(lane >= step, pltpu.roll(total, step, 1), 0)
    first = (total - row)[0:1, :] - start
    return jnp.where(lane[0:1, :] < 64, first, 1 << 20).astype(F32)


def decay_rows(a):
    source = lax.broadcasted_iota(jnp.int32, (128, 128), 0)
    place = lax.broadcasted_iota(jnp.int32, (128, 128), 1)
    low = jnp.where((source < TOK) & (source <= place), 1.0, 0.0).astype(BF16)
    high = jnp.where((source < TOK) & (source + TOK <= place), 1.0, 0.0).astype(BF16)
    before = jnp.zeros((16, 1), F32)
    parts = []
    for pair in range(PEERS // 2):
        part = jnp.dot(a[2 * pair, DEC_ROW : DEC_ROW + 16, :], low, preferred_element_type=F32)
        part += jnp.dot(a[2 * pair + 1, DEC_ROW : DEC_ROW + 16, :], high, preferred_element_type=F32)
        part += before
        before = part[:, 127:128]
        parts.append(part)
    return jnp.concatenate(parts, axis=1) * LOG2E


def gathered(a, index):
    return a[:, index * TOK : (index + 1) * TOK, :].reshape(BLOCK, HEAD)


def state(a, lens, out):
    first = starts(lens)
    last = jnp.max(jnp.where(first <= float(BLOCK - 1), first, -float(1 << 20)), axis=1, keepdims=True)
    sums = decay_rows(a)
    end = sums[:, BLOCK - 1 : BLOCK]
    place = lax.broadcasted_iota(jnp.int32, (16, BLOCK), 1).astype(F32)
    weight = jnp.exp2(jnp.where(place >= last, sums - end, NEVER))
    weight = jnp.transpose(jnp.concatenate([weight, jnp.zeros((112, BLOCK), F32)], axis=0))
    for head in range(HEADS):
        end_keys = (silu(gathered(a, head)).astype(F32) * weight[:, head : head + 1]).astype(BF16)
        total = lax.dot_general(
            end_keys, gathered(a, 4 + head), (((0,), (0,)), ((), ())), preferred_element_type=F32
        )
        out[head * HEAD : (head + 1) * HEAD, :] = total.astype(BF16)
    decay = jnp.broadcast_to(jnp.where(last < 0, jnp.exp2(-end[0:8, :]), 0.0), (8, HEAD))
    high = decay.astype(BF16).astype(F32)
    out[HEADS * HEAD :, :] = jnp.concatenate([high, decay - high], axis=0).astype(BF16)


def prepare(a, lens, cols, rows, kv):
    for index in range(2):
        kv[index * BLOCK : (index + 1) * BLOCK, :] = gathered(a, 8 + index)
    first = starts(lens)
    place = lax.broadcasted_iota(jnp.int32, (BLOCK, 128), 0).astype(F32)
    begin = jnp.max(jnp.where(first <= place, first, -float(1 << 20)), axis=1, keepdims=True)
    sums = decay_rows(a)
    rows[...] = sums
    turned = jnp.transpose(jnp.concatenate([sums, jnp.zeros((112, BLOCK), F32)], axis=0))
    lane = lax.broadcasted_iota(jnp.int32, (BLOCK, HEAD), 1)
    carry = jnp.where(begin < 0, jnp.exp2(-turned), 0.0)
    cols[...] = jnp.where(lane < HEADS, turned, jnp.where(lane == 8, begin, carry))


def within(a, b, cols, rows, mixed_out, highest_out, inside_out, queries, keys, values, bias, maps):
    values[:, HEAD:] = jnp.ones((2 * BLOCK, HEAD), BF16)
    for index, ref in enumerate((keys, values)):
        ref[:BLOCK, :HEAD] = gathered(b, 8 + index)
        ref[BLOCK:, :HEAD] = gathered(a, 8 + index)
    lane = lax.broadcasted_iota(jnp.int32, (ROW_TILE, PART), 1)
    place = lax.broadcasted_iota(jnp.int32, (ROW_TILE, PART), 0).astype(F32)
    for tile in range(BLOCK // ROW_TILE):
        at = slice(tile * ROW_TILE, (tile + 1) * ROW_TILE)
        span = slice(tile * ROW_TILE, tile * ROW_TILE + PART)
        begin = cols[at, 8:9] - float(tile * ROW_TILE)
        source = jnp.where(lane < BLOCK - tile * ROW_TILE, lane - REACH, lane - BLOCK).astype(F32)
        bias[...] = jnp.where((source <= place) & (source >= begin), 0.0, NEVER)
        for head in range(HEADS):
            query = b[2 * tile : 2 * tile + 2, (4 + head) * TOK : (5 + head) * TOK, :].reshape(ROW_TILE, HEAD)
            scores = lax.dot_general(
                query, keys[span, :], (((1,), (1,)), ((), ())), preferred_element_type=F32
            )
            scores = scores * SCALE + bias[...]
            highest = jnp.max(scores, axis=1, keepdims=True)
            weights = jnp.exp2(scores - highest).astype(BF16)
            mixed_out[at, 2 * head * HEAD : 2 * (head + 1) * HEAD] = jnp.dot(
                weights, values[span, :], preferred_element_type=F32
            )
            highest_out[at, head * HEAD : (head + 1) * HEAD] = jnp.broadcast_to(highest, (ROW_TILE, HEAD))

    for head in range(HEADS):
        queries[head * BLOCK : (head + 1) * BLOCK, :] = silu(gathered(b, head))
        maps[head * BLOCK : (head + 1) * BLOCK, :] = silu(gathered(a, head))
    for tile in range(BLOCK // LIN_TILE):
        at = slice(tile * LIN_TILE, (tile + 1) * LIN_TILE)
        width = (tile + 1) * LIN_TILE
        peers = width // TOK
        source = lax.broadcasted_iota(jnp.int32, (LIN_TILE, width), 1).astype(F32)
        place = lax.broadcasted_iota(jnp.int32, (LIN_TILE, width), 0).astype(F32) + float(tile * LIN_TILE)
        allowed = jnp.where((source <= place) & (source >= cols[at, 8:9]), 0.0, NEVER)
        scores = [
            lax.dot_general(
                queries[h * BLOCK + tile * LIN_TILE : h * BLOCK + width, :],
                maps[h * BLOCK : h * BLOCK + width, :],
                (((1,), (1,)), ((), ())),
                preferred_element_type=F32,
            )
            for h in range(HEADS)
        ]
        gaps = [(rows[h : h + 1, :width] - cols[at, h : h + 1]) + allowed for h in range(HEADS)]
        weighted = [(jnp.exp2(gaps[h]) * scores[h]).astype(BF16) for h in range(HEADS)]
        for h in range(HEADS):
            inside_out[at, h * HEAD : (h + 1) * HEAD] = jnp.dot(
                weighted[h],
                a[:peers, (4 + h) * TOK : (5 + h) * TOK, :].reshape(width, HEAD),
                preferred_element_type=F32,
            )


def finish(b, kv1, near, far, cols, mixed_in, highest_in, inside, queries, gain, lin_out, att_out, values, att, lin, done):
    values[:, HEAD:] = jnp.ones((BLOCK, HEAD), BF16)
    values[:, :HEAD] = kv1[BLOCK:, :]
    seen = (lax.broadcasted_iota(jnp.int32, (ROW_TILE, BLOCK), 1) - BLOCK).astype(F32)
    tiles = [slice(tile * ROW_TILE, (tile + 1) * ROW_TILE) for tile in range(BLOCK // ROW_TILE)]
    pieces = [slice(head * HEAD, (head + 1) * HEAD) for head in range(HEADS)]
    copies = []
    for tile, at in enumerate(tiles):
        allowed = jnp.where(seen >= cols[at, 8:9], 0.0, NEVER)
        for head, piece in enumerate(pieces):
            query = b[2 * tile : 2 * tile + 2, (4 + head) * TOK : (5 + head) * TOK, :].reshape(ROW_TILE, HEAD)
            scores = lax.dot_general(
                query,
                kv1[:BLOCK, :],
                (((1,), (1,)), ((), ())),
                preferred_element_type=F32,
            )
            scores = scores * SCALE + allowed
            before = highest_in[at, piece]
            highest = jnp.maximum(jnp.max(scores, axis=1, keepdims=True), before)
            weights = [jnp.exp2(scores[:, c : c + HEAD] - highest).astype(BF16) for c in range(0, BLOCK, HEAD)]
            shrink = jnp.exp2(before - highest)
            mixed = jnp.dot(jnp.concatenate(weights, axis=1), values[...], preferred_element_type=F32)
            first = 2 * head * HEAD
            top = mixed[:, :HEAD] + shrink * mixed_in[at, first : first + HEAD]
            total = mixed[:, HEAD:] + shrink * mixed_in[at, first + HEAD : first + 2 * HEAD]
            att[at, piece] = (top / total).astype(BF16)
        copies.append(pltpu.make_async_copy(att.at[at], att_out.at[at], done.at[tile]))
        copies[-1].start()
    shrink = near[HEADS * HEAD : STATE_ROWS, :].astype(F32)
    shrink = shrink[0:8, :] + shrink[8:16, :]
    incoming = [
        (near[piece, :].astype(F32) + shrink[head : head + 1, :] * far[piece, :].astype(F32)).astype(BF16)
        for head, piece in enumerate(pieces)
    ]
    for tile, at in enumerate(tiles):
        carried = [
            jnp.dot(
                queries[head * BLOCK + tile * ROW_TILE : head * BLOCK + (tile + 1) * ROW_TILE, :],
                incoming[head],
                preferred_element_type=F32,
            )
            for head in range(HEADS)
        ]
        for head, piece in enumerate(pieces):
            combined = inside[at, piece] + carried[head] * cols[at, 4 + head : 5 + head]
            mean = jnp.mean(combined * combined, axis=1, keepdims=True)
            lin[at, piece] = (combined * lax.rsqrt(mean + 1e-6) * gain[:, piece]).astype(BF16)
        copies.append(pltpu.make_async_copy(lin.at[at], lin_out.at[at], done.at[len(tiles) + tile]))
        copies[-1].start()
    for copy in copies:
        copy.wait()


def shifted(block, distance):
    count = lax.axis_size("ctx")
    return lax.ppermute(block, "ctx", [(i, i + distance) for i in range(count - distance)])


def exchanged(packed):
    return lax.all_to_all(packed, "uly", split_axis=0, concat_axis=0, tiled=True)


def shards(q, k, v, decay, gain, lens, aq, ak, av):
    lens = lens.reshape(1, 64)
    fast = lambda dtype, *dims: pltpu.VMEM(dims, dtype)
    shape = lambda *dims: jax.ShapeDtypeStruct(dims, BF16)
    wide, narrow = PEERS * HEADS * HEAD, PEERS * HEAD
    far_core = lambda x: pltpu.with_memory_space_constraint(x, pltpu.HBM)
    in_hbm = pl.BlockSpec(memory_space=pltpu.HBM)
    first, window = call(
        pack_first,
        (shape(PEERS, ROWS_A, HEAD), shape(PEERS, 2 * TOK, HEAD)),
        [
            pltpu.VMEM((TOK, wide), BF16),
            pltpu.VMEM((TOK, wide), BF16),
            pltpu.VMEM((TOK, narrow), BF16),
            pltpu.VMEM((TOK, narrow), BF16),
            pltpu.VMEM((PEERS * HEADS, TOK), BF16),
            pltpu.VMEM((PEERS, ROWS_A, HEAD), BF16),
            pltpu.VMEM((PEERS, 2 * TOK, HEAD), BF16),
            pltpu.SemaphoreType.DMA((5,)),
            pltpu.SemaphoreType.DMA((4,)),
        ],
        [in_hbm] * 5,
        in_hbm,
    )(*(far_core(x) for x in (k, v, ak, av, decay.T)))
    a = near_core(exchanged(first))
    earlier = shifted(window, 2)
    second = call(
        pack_body, pltpu.HBM((PEERS, ROWS_B, HEAD), BF16),
        [pltpu.VMEM((PEERS, 8 * TOK, HEAD), BF16), pltpu.SemaphoreType.DMA], output=in_hbm,
    )(q, aq)
    second = pl.pallas_call(
        insert,
        out_shape=pltpu.HBM((PEERS, ROWS_B, HEAD), BF16),
        in_specs=[pl.BlockSpec(memory_space=pltpu.VMEM), in_hbm],
        out_specs=in_hbm,
        input_output_aliases={1: 0},
        scratch_shapes=[pltpu.SemaphoreType.DMA],
    )(near_core(earlier), far_core(second))
    b = near_core(exchanged(second))
    own = call(state, fast(BF16, STATE_ROWS, HEAD))(a, lens)
    far, near = near_core(shifted(own, 2)), near_core(shifted(own, 1))
    cols, rows, kv = call(
        prepare, (fast(F32, BLOCK, HEAD), fast(F32, 16, BLOCK), fast(BF16, 2 * BLOCK, HEAD))
    )(a, lens)
    kv1 = near_core(shifted(kv, 1))
    cols, rows = near_core(cols), near_core(rows)
    mixed, highest, inside, queries = call(
        within,
        (
            fast(F32, BLOCK, 2 * HEADS * HEAD),
            fast(F32, BLOCK, HEADS * HEAD),
            fast(F32, BLOCK, HEADS * HEAD),
            fast(BF16, HEADS * BLOCK, HEAD),
        ),
        [
            pltpu.VMEM((2 * BLOCK, HEAD), BF16),
            pltpu.VMEM((2 * BLOCK, 2 * HEAD), BF16),
            pltpu.VMEM((ROW_TILE, PART), F32),
            pltpu.VMEM((HEADS * BLOCK, HEAD), BF16),
        ],
    )(a, b, cols, rows)
    lin_out, att_out = call(
        finish,
        (shape(BLOCK, HEADS * HEAD), shape(BLOCK, HEADS * HEAD)),
        [
            pltpu.VMEM((BLOCK, 2 * HEAD), BF16),
            pltpu.VMEM((BLOCK, HEADS * HEAD), BF16),
            pltpu.VMEM((BLOCK, HEADS * HEAD), BF16),
            pltpu.SemaphoreType.DMA((2 * BLOCK // ROW_TILE,)),
        ],
        output=in_hbm,
    )(
        b,
        kv1,
        near,
        far,
        cols,
        near_core(mixed),
        near_core(highest),
        near_core(inside),
        near_core(queries),
        gain.reshape(1, HEADS * HEAD),
    )
    return lin_out, att_out


def solution(mesh):
    rows = P(("ctx", "uly"), None)
    return jax.shard_map(
        shards,
        mesh=mesh,
        in_specs=(rows, rows, rows, rows, P("uly"), P(), rows, rows, rows),
        out_specs=(P("ctx", "uly"), P("ctx", "uly")),
        check_vma=False,
    )
```

```python
import math

import jax
import jax.numpy as jnp
from jax import lax
from jax.experimental import pallas as pl
from jax.experimental.pallas import tpu as pltpu
from jax.sharding import PartitionSpec as P

HEAD = 128
PEERS = 8
TOK = 64
HEADS = 4
BLOCK = PEERS * TOK
REACH = 2 * BLOCK
ROW_TILE = 128
LIN_TILE = 256
PART = BLOCK + ROW_TILE
DEC_ROW = 10 * TOK
ROWS_A = DEC_ROW + 16
ROWS_B = 10 * TOK
STATE_ROWS = HEADS * HEAD + 16
LOG2E = math.log2(math.e)
NEVER = -1e30
SCALE = HEAD ** -0.5 * LOG2E
F32 = jnp.float32
BF16 = jnp.bfloat16
VMEM_LIMIT = 24 * 1024 * 1024


def silu(x):
    half = 0.5 * x.astype(F32)
    return (half + half * jnp.tanh(half)).astype(BF16)


def near_core(x):
    return pltpu.with_memory_space_constraint(x, pltpu.VMEM)


def call(body, out_shape, scratch=(), inputs=None, output=pl.BlockSpec(memory_space=pltpu.VMEM)):
    many = isinstance(out_shape, (tuple, list))
    return pl.pallas_call(
        body,
        out_shape=out_shape,
        **({} if inputs is None else dict(in_specs=inputs)),
        out_specs=tuple(output for _ in out_shape) if many else output,
        scratch_shapes=list(scratch),
        compiler_params=pltpu.CompilerParams(vmem_limit_bytes=VMEM_LIMIT),
    )


def columns(out, source, first, count):
    for peer in range(PEERS):
        for i in range(count):
            column = (peer * count + i) * HEAD
            out[peer, (first + i) * TOK : (first + i + 1) * TOK, :] = source[:, column : column + HEAD]


def pack_first(k, v, ak, av, decay, out, window, k_in, v_in, ak_in, av_in, decay_in, staged, raw, arrived, left):
    pairs = ((ak, ak_in), (av, av_in), (decay, decay_in), (k, k_in), (v, v_in))
    copies = [pltpu.make_async_copy(source, into, arrived.at[i]) for i, (source, into) in enumerate(pairs)]
    for copy in copies:
        copy.start()
    parts = [slice(8 * TOK, ROWS_A), slice(0, 4 * TOK), slice(4 * TOK, 8 * TOK)]
    away = [pltpu.make_async_copy(staged.at[:, part], out.at[:, part], left.at[i]) for i, part in enumerate(parts)]
    away.append(pltpu.make_async_copy(raw, window, left.at[3]))
    copies[0].wait()
    columns(staged, ak_in, 8, 1)
    columns(raw, ak_in, 0, 1)
    copies[1].wait()
    columns(staged, av_in, 9, 1)
    columns(raw, av_in, 1, 1)
    copies[2].wait()
    rows = jnp.concatenate([decay_in[...].astype(F32), jnp.zeros((32, 64), F32)], axis=1)
    for peer in range(PEERS):
        own = rows[HEADS * peer : HEADS * (peer + 1), :]
        own = jnp.concatenate([own, own, jnp.zeros((8, 128), F32)], axis=0)
        staged[peer, DEC_ROW : DEC_ROW + 16, :] = own.astype(BF16)
    away[0].start()
    away[3].start()
    copies[3].wait()
    columns(staged, k_in, 0, HEADS)
    away[1].start()
    copies[4].wait()
    columns(staged, v_in, 4, HEADS)
    away[2].start()
    for copy in away:
        copy.wait()


def pack_second(q, aq, out):
    columns(out, aq, 4, HEADS)
    columns(out, q, 0, HEADS)


def pack_body(q, aq, out, staged, done):
    pack_second(q, aq, staged)
    copy = pltpu.make_async_copy(staged, out.at[:, : 8 * TOK, :], done)
    copy.start()
    copy.wait()


def insert(earlier, packed, out, done):
    copy = pltpu.make_async_copy(earlier, out.at[:, 8 * TOK :, :], done)
    copy.start()
    copy.wait()


def begins(lens):
    start = lax.axis_index("ctx") * BLOCK
    lane = lax.broadcasted_iota(jnp.int32, (8, 128), 1)
    row = jnp.concatenate([lens[...], jnp.zeros((1, 64), jnp.int32)], axis=1)
    row = jnp.broadcast_to(row, (8, 128))
    total = row
    for step in (1, 2, 4, 8, 16, 32):
        total = total + jnp.where(lane >= step, pltpu.roll(total, step, 1), 0)
    first = (total - row)[0:1, :] - start
    first = jnp.where(lane[0:1, :] < 64, first, 1 << 20).astype(F32)
    place = lax.broadcasted_iota(jnp.int32, (BLOCK, 128), 0).astype(F32)
    return jnp.max(jnp.where(first <= place, first, -float(1 << 20)), axis=1, keepdims=True)


def decay_rows(a):
    source = lax.broadcasted_iota(jnp.int32, (128, 128), 0)
    place = lax.broadcasted_iota(jnp.int32, (128, 128), 1)
    low = jnp.where((source < TOK) & (source <= place), 1.0, 0.0).astype(BF16)
    high = jnp.where((source < TOK) & (source + TOK <= place), 1.0, 0.0).astype(BF16)
    before = jnp.zeros((16, 1), F32)
    parts = []
    for pair in range(PEERS // 2):
        part = jnp.dot(a[2 * pair, DEC_ROW : DEC_ROW + 16, :], low, preferred_element_type=F32)
        part += jnp.dot(a[2 * pair + 1, DEC_ROW : DEC_ROW + 16, :], high, preferred_element_type=F32)
        part += before
        before = part[:, 127:128]
        parts.append(part)
    return jnp.concatenate(parts, axis=1) * LOG2E


def gathered(a, index):
    return a[:, index * TOK : (index + 1) * TOK, :].reshape(BLOCK, HEAD)


def state(a, lens, out, cols, rows):
    begin = begins(lens)
    sums = decay_rows(a)
    rows[...] = sums
    turned = jnp.transpose(jnp.concatenate([sums, jnp.zeros((112, BLOCK), F32)], axis=0))
    lane = lax.broadcasted_iota(jnp.int32, (BLOCK, HEAD), 1)
    carry = jnp.where(begin < 0, jnp.exp2(-turned), 0.0)
    cols[...] = jnp.where(lane < HEADS, turned, jnp.where(lane == 8, begin, carry))
    last = begin[BLOCK - 1 : BLOCK, :]
    end = turned[BLOCK - 1 : BLOCK, :]
    place = lax.broadcasted_iota(jnp.int32, (BLOCK, 1), 0).astype(F32)
    weight = jnp.exp2(jnp.where(place >= last, turned - end, NEVER))
    extra = []
    for head in range(HEADS):
        key_map = silu(gathered(a, head))
        end_keys = (key_map.astype(F32) * weight[:, head : head + 1]).astype(BF16)
        total = lax.dot_general(
            end_keys, gathered(a, 4 + head), (((0,), (0,)), ((), ())), preferred_element_type=F32
        )
        out[head * HEAD : (head + 1) * HEAD, :] = total.astype(BF16)
        gone = jnp.where(last < 0, jnp.exp2(-end[:, head : head + 1]), 0.0)
        extra.append(jnp.broadcast_to(gone, (1, HEAD)))
    decay = jnp.concatenate([*extra, jnp.zeros((4, HEAD), F32)], axis=0)
    high = decay.astype(BF16).astype(F32)
    out[HEADS * HEAD :, :] = jnp.concatenate([high, decay - high], axis=0).astype(BF16)


def within(a, b, cols, rows, mixed_out, highest_out, inside_out, queries, keys, values, bias, maps):
    values[:, HEAD:] = jnp.ones((2 * BLOCK, HEAD), BF16)
    for index, ref in enumerate((keys, values)):
        ref[:BLOCK, :HEAD] = gathered(b, 8 + index)
        ref[BLOCK:, :HEAD] = gathered(a, 8 + index)
    lane = lax.broadcasted_iota(jnp.int32, (ROW_TILE, PART), 1)
    place = lax.broadcasted_iota(jnp.int32, (ROW_TILE, PART), 0).astype(F32)
    for tile in range(BLOCK // ROW_TILE):
        at = slice(tile * ROW_TILE, (tile + 1) * ROW_TILE)
        span = slice(tile * ROW_TILE, tile * ROW_TILE + PART)
        begin = cols[at, 8:9] - float(tile * ROW_TILE)
        source = jnp.where(lane < BLOCK - tile * ROW_TILE, lane - REACH, lane - BLOCK).astype(F32)
        bias[...] = jnp.where((source <= place) & (source >= begin), 0.0, NEVER)
        for head in range(HEADS):
            query = b[2 * tile : 2 * tile + 2, (4 + head) * TOK : (5 + head) * TOK, :].reshape(ROW_TILE, HEAD)
            scores = lax.dot_general(
                query, keys[span, :], (((1,), (1,)), ((), ())), preferred_element_type=F32
            )
            scores = scores * SCALE + bias[...]
            highest = jnp.max(scores, axis=1, keepdims=True)
            weights = jnp.exp2(scores - highest).astype(BF16)
            mixed_out[at, 2 * head * HEAD : 2 * (head + 1) * HEAD] = jnp.dot(
                weights, values[span, :], preferred_element_type=F32
            )
            highest_out[at, head * HEAD : (head + 1) * HEAD] = jnp.broadcast_to(highest, (ROW_TILE, HEAD))

    for head in range(HEADS):
        queries[head * BLOCK : (head + 1) * BLOCK, :] = silu(gathered(b, head))
        maps[head * BLOCK : (head + 1) * BLOCK, :] = silu(gathered(a, head))
    for tile in range(BLOCK // LIN_TILE):
        at = slice(tile * LIN_TILE, (tile + 1) * LIN_TILE)
        width = (tile + 1) * LIN_TILE
        peers = width // TOK
        source = lax.broadcasted_iota(jnp.int32, (LIN_TILE, width), 1).astype(F32)
        place = lax.broadcasted_iota(jnp.int32, (LIN_TILE, width), 0).astype(F32) + float(tile * LIN_TILE)
        allowed = jnp.where((source <= place) & (source >= cols[at, 8:9]), 0.0, NEVER)
        scores = [
            lax.dot_general(
                queries[h * BLOCK + tile * LIN_TILE : h * BLOCK + width, :],
                maps[h * BLOCK : h * BLOCK + width, :],
                (((1,), (1,)), ((), ())),
                preferred_element_type=F32,
            )
            for h in range(HEADS)
        ]
        gaps = [(rows[h : h + 1, :width] - cols[at, h : h + 1]) + allowed for h in range(HEADS)]
        weighted = [(jnp.exp2(gaps[h]) * scores[h]).astype(BF16) for h in range(HEADS)]
        for h in range(HEADS):
            inside_out[at, h * HEAD : (h + 1) * HEAD] = jnp.dot(
                weighted[h],
                a[:peers, (4 + h) * TOK : (5 + h) * TOK, :].reshape(width, HEAD),
                preferred_element_type=F32,
            )


def finish(b, kv1, near, far, cols, mixed_in, highest_in, inside, queries, gain, lin_out, att_out, keys, values, att, lin, done):
    values[:, HEAD:] = jnp.ones((BLOCK, HEAD), BF16)
    keys[...] = gathered(kv1, 0)
    values[:, :HEAD] = gathered(kv1, 1)
    seen = (lax.broadcasted_iota(jnp.int32, (ROW_TILE, BLOCK), 1) - BLOCK).astype(F32)
    tiles = [slice(tile * ROW_TILE, (tile + 1) * ROW_TILE) for tile in range(BLOCK // ROW_TILE)]
    pieces = [slice(head * HEAD, (head + 1) * HEAD) for head in range(HEADS)]
    copies = []
    for tile, at in enumerate(tiles):
        allowed = jnp.where(seen >= cols[at, 8:9], 0.0, NEVER)
        for head, piece in enumerate(pieces):
            query = b[2 * tile : 2 * tile + 2, (4 + head) * TOK : (5 + head) * TOK, :].reshape(ROW_TILE, HEAD)
            scores = lax.dot_general(
                query,
                keys[...],
                (((1,), (1,)), ((), ())),
                preferred_element_type=F32,
            )
            scores = scores * SCALE + allowed
            before = highest_in[at, piece]
            highest = jnp.maximum(jnp.max(scores, axis=1, keepdims=True), before)
            weights = [jnp.exp2(scores[:, c : c + HEAD] - highest).astype(BF16) for c in range(0, BLOCK, HEAD)]
            shrink = jnp.exp2(before - highest)
            mixed = jnp.dot(jnp.concatenate(weights, axis=1), values[...], preferred_element_type=F32)
            first = 2 * head * HEAD
            top = mixed[:, :HEAD] + shrink * mixed_in[at, first : first + HEAD]
            total = mixed[:, HEAD:] + shrink * mixed_in[at, first + HEAD : first + 2 * HEAD]
            att[at, piece] = (top / total).astype(BF16)
        copies.append(pltpu.make_async_copy(att.at[at], att_out.at[at], done.at[tile]))
        copies[-1].start()
    shrink = near[HEADS * HEAD : STATE_ROWS, :].astype(F32)
    shrink = shrink[0:8, :] + shrink[8:16, :]
    incoming = [
        (near[piece, :].astype(F32) + shrink[head : head + 1, :] * far[piece, :].astype(F32)).astype(BF16)
        for head, piece in enumerate(pieces)
    ]
    for tile, at in enumerate(tiles):
        carried = [
            jnp.dot(
                queries[head * BLOCK + tile * ROW_TILE : head * BLOCK + (tile + 1) * ROW_TILE, :],
                incoming[head],
                preferred_element_type=F32,
            )
            for head in range(HEADS)
        ]
        for head, piece in enumerate(pieces):
            combined = inside[at, piece] + carried[head] * cols[at, 4 + head : 5 + head]
            mean = jnp.mean(combined * combined, axis=1, keepdims=True)
            lin[at, piece] = (combined * lax.rsqrt(mean + 1e-6) * gain[:, piece]).astype(BF16)
        copies.append(pltpu.make_async_copy(lin.at[at], lin_out.at[at], done.at[len(tiles) + tile]))
        copies[-1].start()
    for copy in copies:
        copy.wait()


def shifted(block, distance):
    count = lax.axis_size("ctx")
    return lax.ppermute(block, "ctx", [(i, i + distance) for i in range(count - distance)])


def exchanged(packed):
    return lax.all_to_all(packed, "uly", split_axis=0, concat_axis=0, tiled=True)


def shards(q, k, v, decay, gain, lens, aq, ak, av):
    lens = lens.reshape(1, 64)
    fast = lambda dtype, *dims: pltpu.VMEM(dims, dtype)
    shape = lambda *dims: jax.ShapeDtypeStruct(dims, BF16)
    wide, narrow = PEERS * HEADS * HEAD, PEERS * HEAD
    far_core = lambda x: pltpu.with_memory_space_constraint(x, pltpu.HBM)
    in_hbm = pl.BlockSpec(memory_space=pltpu.HBM)
    first, window = call(
        pack_first,
        (shape(PEERS, ROWS_A, HEAD), shape(PEERS, 2 * TOK, HEAD)),
        [
            pltpu.VMEM((TOK, wide), BF16),
            pltpu.VMEM((TOK, wide), BF16),
            pltpu.VMEM((TOK, narrow), BF16),
            pltpu.VMEM((TOK, narrow), BF16),
            pltpu.VMEM((PEERS * HEADS, TOK), BF16),
            pltpu.VMEM((PEERS, ROWS_A, HEAD), BF16),
            pltpu.VMEM((PEERS, 2 * TOK, HEAD), BF16),
            pltpu.SemaphoreType.DMA((5,)),
            pltpu.SemaphoreType.DMA((4,)),
        ],
        [in_hbm] * 5,
        in_hbm,
    )(*(far_core(x) for x in (k, v, ak, av, decay.T)))
    a = exchanged(first)
    kv = a[:, 8 * TOK : 10 * TOK, :]
    kv1 = near_core(shifted(kv, 1))
    a = near_core(a)
    earlier = shifted(window, 2)
    second = call(
        pack_body, pltpu.HBM((PEERS, ROWS_B, HEAD), BF16),
        [pltpu.VMEM((PEERS, 8 * TOK, HEAD), BF16), pltpu.SemaphoreType.DMA], output=in_hbm,
    )(q, aq)
    second = pl.pallas_call(
        insert,
        out_shape=pltpu.HBM((PEERS, ROWS_B, HEAD), BF16),
        in_specs=[pl.BlockSpec(memory_space=pltpu.VMEM), in_hbm],
        out_specs=in_hbm,
        input_output_aliases={1: 0},
        scratch_shapes=[pltpu.SemaphoreType.DMA],
    )(near_core(earlier), far_core(second))
    b = near_core(exchanged(second))
    own, cols, rows = call(
        state,
        (
            fast(BF16, STATE_ROWS, HEAD),
            fast(F32, BLOCK, HEAD),
            fast(F32, 16, BLOCK),
        ),
    )(a, lens)
    far, near = near_core(shifted(own, 2)), near_core(shifted(own, 1))
    cols, rows = near_core(cols), near_core(rows)
    mixed, highest, inside, queries = call(
        within,
        (
            fast(F32, BLOCK, 2 * HEADS * HEAD),
            fast(F32, BLOCK, HEADS * HEAD),
            fast(F32, BLOCK, HEADS * HEAD),
            fast(BF16, HEADS * BLOCK, HEAD),
        ),
        [
            pltpu.VMEM((2 * BLOCK, HEAD), BF16),
            pltpu.VMEM((2 * BLOCK, 2 * HEAD), BF16),
            pltpu.VMEM((ROW_TILE, PART), F32),
            pltpu.VMEM((HEADS * BLOCK, HEAD), BF16),
        ],
    )(a, b, cols, rows)
    lin_out, att_out = call(
        finish,
        (shape(BLOCK, HEADS * HEAD), shape(BLOCK, HEADS * HEAD)),
        [
            pltpu.VMEM((BLOCK, HEAD), BF16),
            pltpu.VMEM((BLOCK, 2 * HEAD), BF16),
            pltpu.VMEM((BLOCK, HEADS * HEAD), BF16),
            pltpu.VMEM((BLOCK, HEADS * HEAD), BF16),
            pltpu.SemaphoreType.DMA((2 * BLOCK // ROW_TILE,)),
        ],
        output=in_hbm,
    )(
        b,
        kv1,
        near,
        far,
        cols,
        near_core(mixed),
        near_core(highest),
        near_core(inside),
        near_core(queries),
        gain.reshape(1, HEADS * HEAD),
    )
    return lin_out, att_out


def solution(mesh):
    rows = P(("ctx", "uly"), None)
    return jax.shard_map(
        shards,
        mesh=mesh,
        in_specs=(rows, rows, rows, rows, P("uly"), P(), rows, rows, rows),
        out_specs=(P("ctx", "uly"), P("ctx", "uly")),
        check_vma=False,
    )
```
